512 devices in a mesh: replica: 32 (over z_hi, x, core), tensor: 16 (over z_lo, y).
Axes of the slice: x: 4, y: 8, z: 8 (z_hi: 4, z_lo: 2; z = z_hi * 2 + z_lo), core: 2. Of those that a mesh axis runs over, the one named last changes fastest.
Arguments:
- weights: bfloat16 [32, 8192, 2048], P('replica', 'tensor'), may hold values from -6 to 6
- hidden: bfloat16 [32, 512, 8192], P('replica', None, 'tensor'), may hold values from -6 to 6
- out_grad: bfloat16 [32, 512, 2048], P('replica', None, 'tensor'), may hold values from -0.375 to 0.375
- factor_start: bfloat16 [2, 64, 8192], P(None, None, 'tensor'), may hold values from -6 to 6
- matching: int32 [2], replicated, may hold values from 1 to 31, as said below
Outputs:
- new_weights: bfloat16 [32, 8192, 2048], P('replica', 'tensor')
The draws below stay inside these ranges and needn't reach their ends.
Inputs may be any that keep to these rules, and one draw needn't show every extreme that they name: In step t replica i is matched with replica i XOR matching[t]; in one of the steps matching equals 31.
All inputs are finite; a program needn't handle non-finite values.
Results may differ from the reference program's by a relative error of at most 0.014.
Values may be sent and summed in bfloat16 or wider, within the bound.
A program may use at most 64 MiB of HBM per device.

```python
import jax
import jax.numpy as jnp
from jax import lax

D = 2048
FF = 8192
R = 64
STEPS = 2
TOK = 256
N_REPLICA = 32


def draw_matching(key, part):
    first_key, second_key = jax.random.split(jax.random.fold_in(key, 17))
    others = jax.random.randint(first_key, (STEPS,), 1, N_REPLICA - 1)
    chosen = jax.random.randint(second_key, (), 0, STEPS)
    return jnp.where(jnp.arange(STEPS) == chosen, N_REPLICA - 1, others).astype(jnp.int32)


def levels(key, dims, cuts, smallest, largest):
    loudness = 1.0
    for axis_at, blocks in cuts:
        heights = jax.random.uniform(jax.random.fold_in(jax.random.fold_in(key, 6), axis_at), (blocks,), jnp.float32, smallest / len(cuts), largest / len(cuts))
        loudness = loudness * jnp.repeat(jnp.exp(heights), dims[axis_at] // blocks).reshape((-1,) + (1,) * (len(dims) - 1 - axis_at))
    return loudness


def bell_draw(key, extent, width, bound, shards=(), held_as=jnp.bfloat16):
    loudness = levels(key, extent, shards, -0.22, 0.18) if shards else 1.0
    values = jax.random.normal(key, extent, jnp.float32) * width * loudness
    return jnp.minimum(jnp.maximum(values, -bound), bound).astype(held_as)


def setup_inputs(seed: int = 0) -> dict:
    splits = jax.random.split(jax.random.key(seed), 6)
    weights = bell_draw(splits[0], (N_REPLICA, FF, D), 1.0, 6.0, ((0, 32), (1, 16)))
    hidden = bell_draw(splits[1], (N_REPLICA, STEPS * TOK, FF), 1.0, 6.0, ((0, 32), (2, 16)))
    out_grad = bell_draw(splits[2], (N_REPLICA, STEPS * TOK, D), (1.0 / TOK ** 0.5), 0.375, ((0, 32), (2, 16)))
    factor_start = bell_draw(splits[3], (STEPS, R, FF), 1.0, 6.0, ((2, 16),))
    matching = draw_matching(jax.random.fold_in(splits[5], 71), 0)
    return {"weights": weights, "hidden": hidden, "out_grad": out_grad, "factor_start": factor_start, "matching": matching}


learn_rate = 0.1
momentum_decay = 0.9

def reference(weights, hidden, out_grad, factor_start, matching):
    replica_ids = jnp.arange(N_REPLICA, dtype=jnp.int32)
    current = weights
    momentum = None
    for step_index in range(STEPS):
        hidden_step = hidden[:, step_index * TOK:(step_index + 1) * TOK]
        grads_step = out_grad[:, step_index * TOK:(step_index + 1) * TOK]
        keep_state = step_index + 1 < STEPS
        has_earlier = step_index > 0

        def advance(operands):
            gradient = jnp.dot(operands[0].T.astype(jnp.float32), operands[1].astype(jnp.float32), preferred_element_type=jnp.float32)
            if has_earlier:
                gradient = momentum_decay * operands[3] + gradient
            renewed = (operands[2].astype(jnp.float32) - learn_rate * gradient).astype(jnp.bfloat16)
            if keep_state:
                return (gradient, renewed)
            return renewed
        operand_list = (hidden_step, grads_step, current)
        if has_earlier:
            operand_list = operand_list + (momentum,)
        if keep_state:
            momentum, updated = lax.map(advance, operand_list)
        else:
            updated = lax.map(advance, operand_list)
        start_factor = factor_start[step_index]

        def left_product(weight_rows):
            return jnp.dot(start_factor.astype(jnp.float32), weight_rows.astype(jnp.float32), preferred_element_type=jnp.float32)
        left_all = lax.map(left_product, updated)
        partner = jnp.bitwise_xor(replica_ids, matching[step_index]).astype(jnp.int32)
        left_diff = left_all - left_all[partner]
        gram = jnp.einsum('irk,isk->irs', left_diff, left_diff, precision=lax.Precision.HIGHEST)
        lower_factor = jnp.linalg.cholesky(gram)
        ortho = lax.linalg.triangular_solve(lower_factor, left_diff, left_side=True, lower=True)
        ortho_bf = ortho.astype(jnp.bfloat16)

        def right_product(operands):
            return jnp.dot(operands[0].astype(jnp.float32), operands[1].T.astype(jnp.float32), preferred_element_type=jnp.float32)
        right_all = lax.map(right_product, (ortho_bf, updated))
        right_diff = (right_all - right_all[partner]).astype(jnp.bfloat16)

        def move_half(operands):
            change = jnp.dot(operands[1].T.astype(jnp.float32), operands[2].astype(jnp.float32), preferred_element_type=jnp.float32)
            return (operands[0].astype(jnp.float32) - 0.5 * change).astype(jnp.bfloat16)
        current = lax.map(move_half, (updated, right_diff, ortho_bf))
    return current
```

```python
import functools

import jax
import jax.numpy as jnp
from jax import lax
from jax.experimental import pallas as pl
from jax.experimental.pallas import tpu as pltpu
from jax.sharding import PartitionSpec as P

F32 = jnp.float32
BF = jnp.bfloat16
MESH = pl.DeviceIdType.MESH
RANK = 64
TOK = 256
Y = 8
OFFSETS = [(4, 0), (3, 0), (5, 0), (2, 0), (6, 0), (4, 1), (3, 1), (5, 1), (2, 1), (6, 1), (1, 0), (7, 0), (1, 1), (7, 1), (0, 1)]
CORE_MASKS = [1]
X_MASKS = [2, 4, 6]
Z_MASKS = [8, 16, 24]


def flip(index, mask):
    for bit in range(5):
        if mask >> bit & 1:
            index = index + (1 - 2 * lax.rem(lax.div(index, 2**bit), 2)) * 2**bit
    return index


def nn(a, b):
    return lax.dot_general(a, b, (((1,), (0,)), ((), ())), preferred_element_type=F32)


def nt(a, b):
    return lax.dot_general(a, b, (((1,), (1,)), ((), ())), preferred_element_type=F32)


def tn(a, b):
    return lax.dot_general(a, b, (((0,), (0,)), ((), ())), preferred_element_type=F32)


def inverse_lower_factor(gram):
    n = RANK
    row_at = lax.broadcasted_iota(jnp.int32, (n, n), 0)
    col_at = lax.broadcasted_iota(jnp.int32, (n, n), 1)
    eye = (row_at == col_at).astype(F32)
    wide = jnp.concatenate([gram, eye], axis=1)
    rows = [wide[8 * j : 8 * j + 8] for j in range(8)]
    sub = lax.broadcasted_iota(jnp.int32, (8, 128), 0)

    def spread(block, s):
        return jnp.broadcast_to(block[s : s + 1, :], (8, 128))

    for jb in range(8):
        cols = [
            [jnp.broadcast_to(rows[j][:, 8 * jb + q : 8 * jb + q + 1], (8, 128)) if j >= jb else None for j in range(8)]
            for q in range(8)
        ]
        for s in range(8):
            pivot_row = spread(rows[jb], s)
            inverse = 1.0 / spread(cols[s][jb], s)
            ahead = [spread(cols[q][jb], s) if q > s else None for q in range(8)]
            for j in range(jb, 8):
                factor = cols[s][j] * inverse
                if j == jb:
                    factor = jnp.where(sub > s, factor, 0.0)
                rows[j] = rows[j] - factor * pivot_row
                for q in range(s + 1, 8):
                    cols[q][j] = cols[q][j] - factor * ahead[q]
    wide = jnp.concatenate(rows, axis=0)
    pivots = jnp.sum(wide[:, :n] * eye, axis=1, keepdims=True)
    return wide[:, n:] * lax.rsqrt(pivots)


def orthonormal(diff):
    inverse = inverse_lower_factor(nt(diff, diff))
    high = inverse.astype(BF)
    low = (inverse - high.astype(F32)).astype(BF)
    return nn(jnp.concatenate([high, low], axis=1), jnp.concatenate([diff, diff], axis=0)).astype(BF)


class Sends:
    def __init__(self, send_sems, recv_sems):
        self.send_sems, self.recv_sems = send_sems, recv_sems
        self.count = 0
        self.open = []

    def start(self, copies, total):
        number = self.count
        self.count += 1
        for source, target, device in copies:
            pltpu.make_async_remote_copy(
                src_ref=source,
                dst_ref=target,
                send_sem=self.send_sems.at[number],
                recv_sem=self.recv_sems.at[number],
                device_id=device,
                device_id_type=MESH,
            ).start()
        self.open.append((number, total))
        return number, total

    def wait(self, ticket):
        number, total = ticket
        pltpu.make_async_copy(total, total, self.recv_sems.at[number]).wait()

    def finish(self):
        for number, total in self.open:
            pltpu.make_async_copy(total, total, self.send_sems.at[number]).wait()


class Exchange:
    def __init__(self, sends, replica, tensor, mask, static, bufs):
        self.sends, self.replica, self.tensor = sends, replica, tensor
        self.mask, self.static = mask, static
        self.core, self.xs, self.zs = bufs
        self.ticket = None

    def _send(self, buf, masks):
        copies = [
            (buf.at[0], buf.at[k + 1], (flip(self.replica, mask), self.tensor)) for k, mask in enumerate(masks)
        ]
        self.ticket = self.sends.start(copies, buf.at[pl.ds(1, len(masks))])

    def begin(self, payload):
        self.core[0] = payload
        if self.static is not None:
            self._send(self.core, [self.static])
        else:
            self._send(self.core, CORE_MASKS)

    def along_x(self):
        if self.static is None:
            self.sends.wait(self.ticket)
            self.xs[0] = self.core[lax.rem(self.mask, 2)]
            self._send(self.xs, X_MASKS)

    def along_z(self):
        if self.static is None:
            self.sends.wait(self.ticket)
            self.zs[0] = self.xs[lax.rem(lax.div(self.mask, 2), 4)]
            self._send(self.zs, Z_MASKS)

    def end(self):
        self.sends.wait(self.ticket)
        if self.static is not None:
            return self.core[1]
        return self.zs[lax.rem(lax.div(self.mask, 8), 4)]


def kernel(
    static, m_ref, w_hbm, h_hbm, g_hbm, s_hbm, o_hbm,
    w, h, s, gown, gf, tsend, trecv0, trecv1, tf, zsend, zrecv0, zrecv1, block,
    c0, x0, z0, df0, ef, o0, cl, xl, zl, df1, o1, cr0, xr0, zr0, cr1, xr1, zr1,
    rd0, v, out, send_sems, recv_sems, load_sems, store_sems,
):
    replica = lax.axis_index("replica")
    tensor = lax.axis_index("tensor")
    y = lax.rem(tensor, Y)
    z = lax.div(tensor, Y)

    def at(dy, dz):
        return lax.rem(y + dy + Y, Y) + (z if dz == 0 else 1 - z) * Y

    peers = [(replica, at(dy, dz)) for dy, dz in OFFSETS]
    masks = []
    if None in static:
        masks = CORE_MASKS + X_MASKS + Z_MASKS
    masks = masks + [m for m in set(static) if m is not None]

    barrier = pltpu.get_barrier_semaphore()
    for device in peers + [(flip(replica, mask), tensor) for mask in masks]:
        pl.semaphore_signal(barrier, inc=1, device_id=device, device_id_type=MESH)

    mine = pl.ds(pl.multiple_of(tensor * 128, 128), 128)

    loads = [
        pltpu.make_async_copy(s_hbm, s, load_sems.at[0]),
        pltpu.make_async_copy(h_hbm.at[0], h, load_sems.at[1]),
        pltpu.make_async_copy(w_hbm.at[0], w, load_sems.at[2]),
        pltpu.make_async_copy(g_hbm.at[0], gown, load_sems.at[3]),
        pltpu.make_async_copy(g_hbm.at[0], gf.at[:, mine], load_sems.at[4]),
    ]
    for load in loads:
        load.start()
    loads[0].wait()
    loads[1].wait()
    tsend[...] = nt(h[...], s[...]).astype(BF)
    loads[2].wait()

    def starting_left(i, carry):
        cut = pl.ds(pl.multiple_of(i * 512, 512), 512)
        zsend[:, cut] = nn(s[...], w[:, cut]).astype(BF)
        return carry

    lax.fori_loop(0, 4, starting_left, 0)
    loads[3].wait()
    loads[4].wait()

    pl.semaphore_wait(barrier, len(peers) + len(masks))

    sends = Sends(send_sems, recv_sems)

    def scatter_tokens(step, into):
        copies = []
        for k, (r, t) in enumerate(peers):
            rows = pl.ds(pl.multiple_of(t * 16 + step * TOK, 16), 16)
            copies.append((tsend.at[rows], into.at[k], (r, t)))
        return sends.start(copies, into)

    def scatter_columns(step, into):
        copies = []
        for k, (r, t) in enumerate(peers):
            cut = pl.ds(pl.multiple_of(t * 128, 128), 128)
            copies.append((zsend.at[pl.ds(step * RANK, RANK), cut], into.at[k], (r, t)))
        return sends.start(copies, into)

    def gather_columns(source, into):
        return sends.start([(source, into.at[:, mine], p) for p in peers], into.at[:, pl.ds(0, 15 * 128)])

    def sum_tokens(step, arrived):
        rows = pl.ds(pl.multiple_of(tensor * 16 + step * TOK, 16), 16)
        total = tsend[rows].astype(F32)
        for k in range(15):
            total = total + arrived[k].astype(F32)
        tf[rows] = total.astype(BF)
        return sends.start([(tf.at[rows], tf.at[rows], p) for p in peers], tf.at[pl.ds(0, 15 * 16)])

    def sum_columns(step, arrived):
        total = zsend[pl.ds(step * RANK, RANK), mine].astype(F32)
        for k in range(15):
            total = total + arrived[k].astype(F32)
        return total

    gshard = gown

    def forward(dy_from, dz, dy_to):
        cut = pl.ds(pl.multiple_of(at(dy_from, dz) * 128, 128), 128)
        source = gown if (dy_from, dz) == (0, 0) else gf.at[:, cut]
        return sends.start([(source, gf.at[:, cut], (replica, at(dy_to, 0)))], gshard)

    t0 = scatter_tokens(0, trecv0)
    q0 = scatter_columns(0, zrecv0)
    t1 = scatter_tokens(1, trecv1)
    q1 = scatter_columns(1, zrecv1)
    gz = sends.start([(gown, gf.at[:, mine], (replica, at(0, 1)))], gshard)
    ra = forward(0, 0, 1)
    la = forward(0, 0, -1)

    sends.wait(t0)
    t0 = sum_tokens(0, trecv0)
    sends.wait(t1)
    t1 = sum_tokens(1, trecv1)
    sends.wait(q0)
    left0 = sum_columns(0, zrecv0)
    sends.wait(q1)
    left1 = sum_columns(1, zrecv1)
    sends.wait(t0)
    grad0 = tn(tf[pl.ds(0, TOK)], gown[pl.ds(0, TOK)])
    y0 = (left0 - 0.1 * grad0[:RANK]).astype(BF)
    x1 = left1 - 0.1 * grad0[RANK:]

    first = Exchange(sends, replica, tensor, m_ref[0], static[0], (c0, x0, z0))
    first.begin(jnp.concatenate([y0, x1.astype(BF)], axis=0))
    sends.wait(gz)
    rb = forward(0, 1, 1)
    lb = forward(0, 1, -1)
    first.along_x()
    sends.wait(ra)
    ra = forward(-1, 0, 1)
    sends.wait(la)
    la = forward(1, 0, -1)
    sends.wait(t1)
    grad1 = tn(tf[pl.ds(TOK, TOK)], gown[pl.ds(TOK, TOK)])
    y1 = x1 - 0.09 * grad0[RANK:] - 0.1 * grad1[RANK:]
    first.along_z()
    sends.wait(rb)
    rb = forward(-1, 1, 1)
    sends.wait(lb)
    lb = forward(1, 1, -1)
    other = first.end()
    diff = (y0.astype(F32) - other[:RANK].astype(F32)).astype(BF)
    both = (x1 + other[RANK:].astype(F32)).astype(BF)
    block[0] = diff
    block[1] = both
    df0[:, mine] = diff
    ef[:, mine] = both
    d0 = gather_columns(block.at[0], df0)
    e0 = gather_columns(block.at[1], ef)
    sends.wait(ra)
    ra = forward(-2, 0, 1)
    sends.wait(la)
    la = forward(2, 0, -1)
    sends.wait(d0)
    o0[...] = orthonormal(df0[...])
    sends.wait(e0)
    moved = nt(ef[...], o0[...]).astype(BF)
    l1 = (y1 - 0.5 * nn(moved, o0[:, mine])).astype(BF)

    second = Exchange(sends, replica, tensor, m_ref[1], static[1], (cl, xl, zl))
    second.begin(l1)
    sends.wait(rb)
    rb = forward(-2, 1, 1)
    sends.wait(lb)
    lb = forward(2, 1, -1)
    second.along_x()
    sends.wait(ra)
    ra = forward(-3, 0, 1)
    sends.wait(la)
    sends.wait(rb)
    sends.wait(lb)
    lb = forward(3, 1, -1)
    second.along_z()
    sends.wait(ra)
    sends.wait(lb)
    r0 = nt(o0[...], w[...]) - 0.1 * nn(nt(o0[...], gf[pl.ds(0, TOK)]).astype(BF), h[pl.ds(0, TOK)])
    r0 = r0.astype(BF)
    right0 = Exchange(sends, replica, tensor, m_ref[0], static[0], (cr0, xr0, zr0))
    right0.begin(r0)
    diff = (l1.astype(F32) - second.end().astype(F32)).astype(BF)
    block[2] = diff
    df1[:, mine] = diff
    d1 = gather_columns(block.at[2], df1)
    right0.along_x()
    right0.along_z()

    def settled(i, carry):
        cut = pl.ds(pl.multiple_of(i * 256, 256), 256)
        early = tn(h[pl.ds(0, TOK)], gf[pl.ds(0, TOK), cut])
        late = tn(h[pl.ds(TOK, TOK)], gf[pl.ds(TOK, TOK), cut])
        v[:, cut] = w[:, cut].astype(F32) - 0.19 * early - 0.1 * late
        return carry

    sends.wait(d1)
    o1[...] = orthonormal(df1[...])
    grad_part = nt(o1[...], gf[...])
    grad_part = jnp.concatenate([0.19 * grad_part[:, :TOK], 0.1 * grad_part[:, TOK:]], axis=1).astype(BF)
    cross = (0.5 * nt(o1[...], o0[...])).astype(BF)
    r1 = nt(o1[...], w[...]) - nn(grad_part, h[...])
    diff0 = (r0.astype(F32) - right0.end().astype(F32)).astype(BF)
    rd0[...] = diff0
    r1 = (r1 - nn(cross, diff0)).astype(BF)
    right1 = Exchange(sends, replica, tensor, m_ref[1], static[1], (cr1, xr1, zr1))
    right1.begin(r1)
    right1.along_x()
    lax.fori_loop(0, 4, settled, 0)
    right1.along_z()
    lax.fori_loop(4, 8, settled, 0)

    def first_move(i, carry):
        cut = pl.ds(pl.multiple_of(i * 256, 256), 256)
        v[:, cut] = v[:, cut] - 0.5 * tn(rd0[...], o0[:, cut])
        return carry

    lax.fori_loop(0, 8, first_move, 0)
    diff1 = (r1.astype(F32) - right1.end().astype(F32)).astype(BF)
    stores = []
    for i in range(4):
        rows = pl.ds(128 * i, 128)
        out[rows] = (v[rows] - 0.5 * tn(diff1[:, 128 * i : 128 * i + 128], o1[...])).astype(BF)
        store = pltpu.make_async_copy(out.at[rows], o_hbm.at[0, rows], store_sems.at[i])
        store.start()
        stores.append(store)
    sends.finish()
    for store in stores:
        store.wait()


def steps(static, number, matching, weights, hidden, out_grad, factors):
    def bf(*shape):
        return pltpu.VMEM(shape, BF)

    anywhere = pl.BlockSpec(memory_space=pl.ANY)
    return pl.pallas_call(
        functools.partial(kernel, static),
        out_shape=jax.ShapeDtypeStruct(weights.shape, BF),
        in_specs=[pl.BlockSpec(memory_space=pltpu.SMEM)] + [anywhere] * 4,
        out_specs=anywhere,
        scratch_shapes=[
            bf(512, 2048), bf(512, 512), bf(128, 512), bf(512, 128), bf(512, 2048),
            bf(512, 128), bf(15, 16, 128), bf(15, 16, 128), bf(512, 128),
            bf(128, 2048), bf(15, 64, 128), bf(15, 64, 128), bf(3, 64, 128),
            bf(2, 128, 128), bf(4, 128, 128), bf(4, 128, 128), bf(64, 2048), bf(64, 2048), bf(64, 2048),
            bf(2, 64, 128), bf(4, 64, 128), bf(4, 64, 128), bf(64, 2048), bf(64, 2048),
            bf(2, 64, 512), bf(4, 64, 512), bf(4, 64, 512),
            bf(2, 64, 512), bf(4, 64, 512), bf(4, 64, 512),
            bf(64, 512), pltpu.VMEM((512, 2048), F32), bf(512, 2048),
            pltpu.SemaphoreType.DMA((48,)), pltpu.SemaphoreType.DMA((48,)),
            pltpu.SemaphoreType.DMA((5,)), pltpu.SemaphoreType.DMA((4,)),
        ],
        compiler_params=pltpu.CompilerParams(
            collective_id=number, has_side_effects=True, vmem_limit_bytes=48 << 20
        ),
        name="gossip_steps",
    )(matching, weights, hidden, out_grad, factors)


def per_device(weights, hidden, out_grad, factor_start, matching):
    factors = factor_start.reshape(2 * RANK, factor_start.shape[2])
    return steps((None, None), 0, matching, weights, hidden, out_grad, factors)


def solution(mesh):
    return jax.shard_map(
        per_device,
        mesh=mesh,
        in_specs=(
            P("replica", "tensor", None),
            P("replica", None, "tensor"),
            P("replica", None, "tensor"),
            P(None, None, "tensor"),
            P(),
        ),
        out_specs=P("replica", "tensor", None),
        check_vma=False,
    )
```

```python
import functools

import jax
import jax.numpy as jnp
from jax import lax
from jax.experimental import pallas as pl
from jax.experimental.pallas import tpu as pltpu
from jax.sharding import PartitionSpec as P

F32 = jnp.float32
BF = jnp.bfloat16
MESH = pl.DeviceIdType.MESH
RANK = 64
TOK = 256
Y = 8
OFFSETS = [(4, 0), (3, 0), (5, 0), (2, 0), (6, 0), (4, 1), (3, 1), (5, 1), (2, 1), (6, 1), (1, 0), (7, 0), (1, 1), (7, 1), (0, 1)]
CORE_MASKS = [1]
X_MASKS = [2, 4, 6]
Z_MASKS = [8, 16, 24]


def flip(index, mask):
    for bit in range(5):
        if mask >> bit & 1:
            index = index + (1 - 2 * lax.rem(lax.div(index, 2**bit), 2)) * 2**bit
    return index


def nn(a, b):
    return lax.dot_general(a, b, (((1,), (0,)), ((), ())), preferred_element_type=F32)


def nt(a, b):
    return lax.dot_general(a, b, (((1,), (1,)), ((), ())), preferred_element_type=F32)


def tn(a, b):
    return lax.dot_general(a, b, (((0,), (0,)), ((), ())), preferred_element_type=F32)


def inverse_lower_factor(gram):
    n = RANK
    row_at = lax.broadcasted_iota(jnp.int32, (n, n), 0)
    col_at = lax.broadcasted_iota(jnp.int32, (n, n), 1)
    eye = (row_at == col_at).astype(F32)
    wide = jnp.concatenate([gram, eye], axis=1)
    rows = [wide[8 * j : 8 * j + 8] for j in range(8)]
    sub = lax.broadcasted_iota(jnp.int32, (8, 128), 0)

    def spread(block, s):
        return jnp.broadcast_to(block[s : s + 1, :], (8, 128))

    for jb in range(8):
        cols = [
            [jnp.broadcast_to(rows[j][:, 8 * jb + q : 8 * jb + q + 1], (8, 128)) if j >= jb else None for j in range(8)]
            for q in range(8)
        ]
        for s in range(8):
            pivot_row = spread(rows[jb], s)
            inverse = 1.0 / spread(cols[s][jb], s)
            ahead = [spread(cols[q][jb], s) if q > s else None for q in range(8)]
            for j in range(jb, 8):
                factor = cols[s][j] * inverse
                if j == jb:
                    factor = jnp.where(sub > s, factor, 0.0)
                rows[j] = rows[j] - factor * pivot_row
                for q in range(s + 1, 8):
                    cols[q][j] = cols[q][j] - factor * ahead[q]
    wide = jnp.concatenate(rows, axis=0)
    pivots = jnp.sum(wide[:, :n] * eye, axis=1, keepdims=True)
    return wide[:, n:] * lax.rsqrt(pivots)


def split(value):
    high = value.astype(BF)
    return high, (value - high.astype(F32)).astype(BF)


def split_nn(a, b):
    high, low = split(a)
    if b.dtype == BF:
        return nn(jnp.concatenate([high, low], axis=1), jnp.concatenate([b, b], axis=0))
    b_high, b_low = split(b)
    return nn(jnp.concatenate([high, low, high], axis=1), jnp.concatenate([b_high, b_high, b_low], axis=0))


def orthonormal(diff):
    return split_nn(inverse_lower_factor(nt(diff, diff)), diff).astype(BF)


class Sends:
    def __init__(self, send_sems, recv_sems):
        self.send_sems, self.recv_sems = send_sems, recv_sems
        self.count = 0
        self.open = []

    def start(self, copies, total):
        number = self.count
        self.count += 1
        for source, target, device in copies:
            pltpu.make_async_remote_copy(
                src_ref=source,
                dst_ref=target,
                send_sem=self.send_sems.at[number],
                recv_sem=self.recv_sems.at[number],
                device_id=device,
                device_id_type=MESH,
            ).start()
        self.open.append((number, total))
        return number, total

    def wait(self, ticket):
        number, total = ticket
        pltpu.make_async_copy(total, total, self.recv_sems.at[number]).wait()

    def finish(self):
        for number, total in self.open:
            pltpu.make_async_copy(total, total, self.send_sems.at[number]).wait()


class Exchange:
    def __init__(self, sends, replica, tensor, mask, static, bufs):
        self.sends, self.replica, self.tensor = sends, replica, tensor
        self.mask, self.static = mask, static
        self.core, self.xs, self.zs = bufs
        self.ticket = None

    def _send(self, buf, masks):
        copies = [
            (buf.at[0], buf.at[k + 1], (flip(self.replica, mask), self.tensor)) for k, mask in enumerate(masks)
        ]
        self.ticket = self.sends.start(copies, buf.at[pl.ds(1, len(masks))])

    def begin(self, payload):
        self.core[0] = payload
        if self.static is not None:
            self._send(self.core, [self.static])
        else:
            self._send(self.core, CORE_MASKS)

    def along_x(self):
        if self.static is None:
            self.sends.wait(self.ticket)
            self.xs[0] = self.core[lax.rem(self.mask, 2)]
            self._send(self.xs, X_MASKS)

    def along_z(self):
        if self.static is None:
            self.sends.wait(self.ticket)
            self.zs[0] = self.xs[lax.rem(lax.div(self.mask, 2), 4)]
            self._send(self.zs, Z_MASKS)

    def end(self):
        self.sends.wait(self.ticket)
        if self.static is not None:
            return self.core[1]
        return self.zs[lax.rem(lax.div(self.mask, 8), 4)]


def kernel(
    static, m_ref, w_hbm, h_hbm, g_hbm, s_hbm, o_hbm,
    w, h, s, gown, gf, tsend, trecv0, trecv1, tf, zsend, zrecv0, zrecv1, block,
    c0, x0, z0, ce, xe, ze, df0, ef, o0, cl, xl, zl, df1, o1, cr0, xr0, zr0, cr1, xr1, zr1,
    rd0, v, out, send_sems, recv_sems, load_sems, store_sems,
):
    replica = lax.axis_index("replica")
    tensor = lax.axis_index("tensor")
    y = lax.rem(tensor, Y)
    z = lax.div(tensor, Y)

    def at(dy, dz):
        return lax.rem(y + dy + Y, Y) + (z if dz == 0 else 1 - z) * Y

    peers = [(replica, at(dy, dz)) for dy, dz in OFFSETS]
    masks = []
    if None in static:
        masks = CORE_MASKS + X_MASKS + Z_MASKS
    masks = masks + [m for m in set(static) if m is not None]

    barrier = pltpu.get_barrier_semaphore()
    for device in peers + [(flip(replica, mask), tensor) for mask in masks]:
        pl.semaphore_signal(barrier, inc=1, device_id=device, device_id_type=MESH)

    mine = pl.ds(pl.multiple_of(tensor * 128, 128), 128)

    loads = [
        pltpu.make_async_copy(s_hbm, s, load_sems.at[0]),
        pltpu.make_async_copy(h_hbm.at[0], h, load_sems.at[1]),
        pltpu.make_async_copy(w_hbm.at[0], w, load_sems.at[2]),
        pltpu.make_async_copy(g_hbm.at[0], gown, load_sems.at[3]),
        pltpu.make_async_copy(g_hbm.at[0], gf.at[:, mine], load_sems.at[4]),
    ]
    for load in loads:
        load.start()
    loads[0].wait()
    loads[1].wait()
    tsend[...] = nt(h[...], s[...]).astype(BF)
    loads[2].wait()

    def starting_left(i, carry):
        cut = pl.ds(pl.multiple_of(i * 512, 512), 512)
        zsend[:, cut] = nn(s[...], w[:, cut]).astype(BF)
        return carry

    lax.fori_loop(0, 4, starting_left, 0)
    pl.semaphore_wait(barrier, len(peers) + len(masks))

    sends = Sends(send_sems, recv_sems)

    def scatter_tokens(step, into):
        copies = []
        for k, (r, t) in enumerate(peers):
            rows = pl.ds(pl.multiple_of(t * 16 + step * TOK, 16), 16)
            copies.append((tsend.at[rows], into.at[k], (r, t)))
        return sends.start(copies, into)

    def scatter_columns(step, into):
        copies = []
        for k, (r, t) in enumerate(peers):
            cut = pl.ds(pl.multiple_of(t * 128, 128), 128)
            copies.append((zsend.at[pl.ds(step * RANK, RANK), cut], into.at[k], (r, t)))
        return sends.start(copies, into)

    def gather_columns(source, into):
        return sends.start([(source, into.at[:, mine], p) for p in peers], into.at[:, pl.ds(0, 15 * 128)])

    def sum_tokens(step, arrived):
        rows = pl.ds(pl.multiple_of(tensor * 16 + step * TOK, 16), 16)
        total = tsend[rows].astype(F32)
        for k in range(15):
            total = total + arrived[k].astype(F32)
        tf[rows] = total.astype(BF)
        return sends.start([(tf.at[rows], tf.at[rows], p) for p in peers], tf.at[pl.ds(0, 15 * 16)])

    def sum_columns(step, arrived):
        total = zsend[pl.ds(step * RANK, RANK), mine].astype(F32)
        for k in range(15):
            total = total + arrived[k].astype(F32)
        return total

    ring = {}

    def shard(dy, dz, to_dy, to_dz):
        cut = pl.ds(pl.multiple_of(at(dy, dz) * 128, 128), 128)
        source = gown if (dy, dz) == (0, 0) else gf.at[:, cut]
        return sends.start([(source, gf.at[:, cut], (replica, at(to_dy, to_dz)))], gown)

    def right(dy, dz):
        ring[dy - 1, dz] = shard(dy, dz, 1, 0)

    def left(dy, dz):
        ring[dy + 1, dz] = shard(dy, dz, -1, 0)

    def across(dy):
        ring[dy, 1] = shard(dy, 0, 0, 1)

    def arrived(dy, dz):
        sends.wait(ring.pop((dy, dz)))

    def pump0():
        right(0, 0)
        left(0, 0)
        across(0)

    def pump1():
        arrived(-1, 0)
        right(-1, 0)
        arrived(1, 0)
        left(1, 0)
        across(-1)
        across(1)

    def pump2():
        arrived(-2, 0)
        right(-2, 0)
        arrived(2, 0)
        left(2, 0)
        across(-2)
        across(2)

    def pump3():
        arrived(-3, 0)
        right(-3, 0)
        arrived(-2, 1)
        right(-2, 1)
        arrived(2, 1)
        left(2, 1)

    def pump4():
        arrived(3, 1)
        left(3, 1)

    def pump5():
        for place in list(ring):
            arrived(*place)

    early = static[0] is not None

    t0 = scatter_tokens(0, trecv0)
    q0 = scatter_columns(0, zrecv0)
    sends.wait(t0)
    t0 = sum_tokens(0, trecv0)
    q1 = scatter_columns(1, zrecv1)
    t1 = scatter_tokens(1, trecv1)
    loads[3].wait()
    loads[4].wait()
    pump0()
    sends.wait(q0)
    left0 = sum_columns(0, zrecv0)
    sends.wait(t0)
    grad0 = tn(tf[pl.ds(0, TOK)], gown[pl.ds(0, TOK)])
    y0 = (left0 - 0.1 * grad0[:RANK]).astype(BF)
    first = Exchange(sends, replica, tensor, m_ref[0], static[0], (c0, x0, z0))
    cross = Exchange(sends, replica, tensor, m_ref[0], static[0], (ce, xe, ze))
    first.begin(y0)
    first.along_x()
    sends.wait(q1)
    x1 = sum_columns(1, zrecv1) - 0.1 * grad0[RANK:]
    cross.begin(x1.astype(BF))
    if early:
        pump1()
    sends.wait(t1)
    t1 = sum_tokens(1, trecv1)
    first.along_z()
    cross.along_x()
    if not early:
        pump1()
    diff = (y0.astype(F32) - first.end().astype(F32)).astype(BF)
    block[0] = diff
    df0[:, mine] = diff
    d0 = gather_columns(block.at[0], df0)
    cross.along_z()
    both = (x1 + cross.end().astype(F32)).astype(BF)
    block[1] = both
    ef[:, mine] = both
    e0 = gather_columns(block.at[1], ef)
    pump2()
    sends.wait(t1)
    grad1 = tn(tf[pl.ds(TOK, TOK)], gown[pl.ds(TOK, TOK)])
    y1 = x1 - 0.09 * grad0[RANK:] - 0.1 * grad1[RANK:]
    sends.wait(d0)
    o0[...] = orthonormal(df0[...])
    if not early:
        pump3()
    sends.wait(e0)
    moved = nt(ef[...], o0[...]).astype(BF)
    l1 = (y1 - 0.5 * nn(moved, o0[:, mine])).astype(BF)
    second = Exchange(sends, replica, tensor, m_ref[1], static[1], (cl, xl, zl))
    second.begin(l1)
    second.along_x()
    if early:
        pump3()
    second.along_z()
    pump4()
    diff = (l1.astype(F32) - second.end().astype(F32)).astype(BF)
    block[2] = diff
    df1[:, mine] = diff
    d1 = gather_columns(block.at[2], df1)
    pump5()
    r0 = nt(o0[...], w[...]) - 0.1 * nn(nt(o0[...], gf[pl.ds(0, TOK)]).astype(BF), h[pl.ds(0, TOK)])
    r0 = r0.astype(BF)
    right0 = Exchange(sends, replica, tensor, m_ref[0], static[0], (cr0, xr0, zr0))
    right0.begin(r0)
    right0.along_x()

    def settled(i, carry):
        cut = pl.ds(pl.multiple_of(i * 256, 256), 256)
        older = tn(h[pl.ds(0, TOK)], gf[pl.ds(0, TOK), cut])
        newer = tn(h[pl.ds(TOK, TOK)], gf[pl.ds(TOK, TOK), cut])
        v[:, cut] = w[:, cut].astype(F32) - 0.19 * older - 0.1 * newer
        return carry

    lax.fori_loop(0, 8, settled, 0)
    right0.along_z()
    sends.wait(d1)
    d1_all = df1[...]
    grad_part = nt(d1_all, gf[...])
    grad_part = jnp.concatenate([0.19 * grad_part[:, :TOK], 0.1 * grad_part[:, TOK:]], axis=1).astype(BF)
    mixed = (0.5 * nt(d1_all, o0[...])).astype(BF)
    k1 = nt(d1_all, w[...]) - nn(grad_part, h[...])
    diff0 = (r0.astype(F32) - right0.end().astype(F32)).astype(BF)
    rd0[...] = diff0
    k1 = (k1 - nn(mixed, diff0)).astype(BF)
    right1 = Exchange(sends, replica, tensor, m_ref[1], static[1], (cr1, xr1, zr1))
    right1.begin(k1)
    right1.along_x()
    inverse = inverse_lower_factor(nt(d1_all, d1_all))
    o1[...] = split_nn(inverse, d1_all).astype(BF)
    right1.along_z()

    def first_move(i, carry):
        cut = pl.ds(pl.multiple_of(i * 256, 256), 256)
        v[:, cut] = v[:, cut] - 0.5 * tn(rd0[...], o0[:, cut])
        return carry

    lax.fori_loop(0, 8, first_move, 0)
    apart = k1.astype(F32) - right1.end().astype(F32)
    rd1 = split_nn(inverse, apart).astype(BF)
    stores = []
    for i in range(4):
        rows = pl.ds(128 * i, 128)
        out[rows] = (v[rows] - 0.5 * tn(rd1[:, 128 * i : 128 * i + 128], o1[...])).astype(BF)
        store = pltpu.make_async_copy(out.at[rows], o_hbm.at[0, rows], store_sems.at[i])
        store.start()
        stores.append(store)
    sends.finish()
    for store in stores:
        store.wait()


def steps(static, number, matching, weights, hidden, out_grad, factors):
    def bf(*shape):
        return pltpu.VMEM(shape, BF)

    anywhere = pl.BlockSpec(memory_space=pl.ANY)
    return pl.pallas_call(
        functools.partial(kernel, static),
        out_shape=jax.ShapeDtypeStruct(weights.shape, BF),
        in_specs=[pl.BlockSpec(memory_space=pltpu.SMEM)] + [anywhere] * 4,
        out_specs=anywhere,
        scratch_shapes=[
            bf(512, 2048), bf(512, 512), bf(128, 512), bf(512, 128), bf(512, 2048),
            bf(512, 128), bf(15, 16, 128), bf(15, 16, 128), bf(512, 128),
            bf(128, 2048), bf(15, 64, 128), bf(15, 64, 128), bf(3, 64, 128),
            bf(2, 64, 128), bf(4, 64, 128), bf(4, 64, 128), bf(2, 64, 128), bf(4, 64, 128), bf(4, 64, 128),
            bf(64, 2048), bf(64, 2048), bf(64, 2048),
            bf(2, 64, 128), bf(4, 64, 128), bf(4, 64, 128), bf(64, 2048), bf(64, 2048),
            bf(2, 64, 512), bf(4, 64, 512), bf(4, 64, 512),
            bf(2, 64, 512), bf(4, 64, 512), bf(4, 64, 512),
            bf(64, 512), pltpu.VMEM((512, 2048), F32), bf(512, 2048),
            pltpu.SemaphoreType.DMA((48,)), pltpu.SemaphoreType.DMA((48,)),
            pltpu.SemaphoreType.DMA((5,)), pltpu.SemaphoreType.DMA((4,)),
        ],
        compiler_params=pltpu.CompilerParams(
            collective_id=number, has_side_effects=True, vmem_limit_bytes=60 << 20
        ),
        name="gossip_steps",
    )(matching, weights, hidden, out_grad, factors)


def per_device(weights, hidden, out_grad, factor_start, matching):
    factors = factor_start.reshape(2 * RANK, factor_start.shape[2])
    return lax.cond(
        matching[0] == 31,
        functools.partial(steps, (31, None), 0),
        functools.partial(steps, (None, 31), 1),
        matching, weights, hidden, out_grad, factors,
    )


def solution(mesh):
    return jax.shard_map(
        per_device,
        mesh=mesh,
        in_specs=(
            P("replica", "tensor", None),
            P("replica", None, "tensor"),
            P("replica", None, "tensor"),
            P(None, None, "tensor"),
            P(),
        ),
        out_specs=P("replica", "tensor", None),
        check_vma=False,
    )
```

```python
import functools

import jax
import jax.numpy as jnp
from jax import lax
from jax.experimental import pallas as pl
from jax.experimental.pallas import tpu as pltpu
from jax.sharding import PartitionSpec as P

F32 = jnp.float32
BF = jnp.bfloat16
MESH = pl.DeviceIdType.MESH
RANK = 64
TOK = 256
Y = 8
OFFSETS = [(4, 0), (3, 0), (5, 0), (2, 0), (6, 0), (4, 1), (3, 1), (5, 1), (2, 1), (6, 1), (1, 0), (7, 0), (1, 1), (7, 1), (0, 1)]
CORE_MASKS = [1]
X_MASKS = [2, 4, 6]
Z_MASKS = [8, 16, 24]


PLANS = [
    (["on", "on", "", "", "on", "", "on", "on", "on", "", ""], 8),
    (["o", "on", "on", "o", "o", "no", "n", "", "", "n", "n"], 5),
]


def flip(index, mask):
    for bit in range(5):
        if mask >> bit & 1:
            index = index + (1 - 2 * lax.rem(lax.div(index, 2**bit), 2)) * 2**bit
    return index


def nn(a, b):
    return lax.dot_general(a, b, (((1,), (0,)), ((), ())), preferred_element_type=F32)


def nt(a, b):
    return lax.dot_general(a, b, (((1,), (1,)), ((), ())), preferred_element_type=F32)


def tn(a, b):
    return lax.dot_general(a, b, (((0,), (0,)), ((), ())), preferred_element_type=F32)


def inverse_lower_factor(gram):
    n = RANK
    row_at = lax.broadcasted_iota(jnp.int32, (n, n), 0)
    col_at = lax.broadcasted_iota(jnp.int32, (n, n), 1)
    eye = (row_at == col_at).astype(F32)
    wide = jnp.concatenate([gram, eye], axis=1)
    rows = [wide[8 * j : 8 * j + 8] for j in range(8)]
    sub = lax.broadcasted_iota(jnp.int32, (8, 128), 0)

    def spread(block, s):
        return jnp.broadcast_to(block[s : s + 1, :], (8, 128))

    for jb in range(8):
        cols = [
            [jnp.broadcast_to(rows[j][:, 8 * jb + q : 8 * jb + q + 1], (8, 128)) if j >= jb else None for j in range(8)]
            for q in range(8)
        ]
        for s in range(8):
            pivot_row = spread(rows[jb], s)
            inverse = 1.0 / spread(cols[s][jb], s)
            ahead = [spread(cols[q][jb], s) if q > s else None for q in range(8)]
            for j in range(jb, 8):
                factor = cols[s][j] * inverse
                if j == jb:
                    factor = jnp.where(sub > s, factor, 0.0)
                rows[j] = rows[j] - factor * pivot_row
                for q in range(s + 1, 8):
                    cols[q][j] = cols[q][j] - factor * ahead[q]
    wide = jnp.concatenate(rows, axis=0)
    pivots = jnp.sum(wide[:, :n] * eye, axis=1, keepdims=True)
    return wide[:, n:] * lax.rsqrt(pivots)


def split(value):
    high = value.astype(BF)
    return high, (value - high.astype(F32)).astype(BF)


def split_nn(a, b):
    high, low = split(a)
    if b.dtype == BF:
        return nn(jnp.concatenate([high, low], axis=1), jnp.concatenate([b, b], axis=0))
    b_high, b_low = split(b)
    return nn(jnp.concatenate([high, low, high], axis=1), jnp.concatenate([b_high, b_high, b_low], axis=0))


def split_nt(a, b):
    a_high, a_low = split(a)
    b_high, b_low = split(b)
    return nt(jnp.concatenate([a_high, a_low, a_high], axis=1), jnp.concatenate([b_high, b_high, b_low], axis=1))


class Sends:
    def __init__(self, send_sems, recv_sems):
        self.send_sems, self.recv_sems = send_sems, recv_sems
        self.count = 0
        self.open = []

    def start(self, copies, total):
        number = self.count
        self.count += 1
        for source, target, device in copies:
            pltpu.make_async_remote_copy(
                src_ref=source,
                dst_ref=target,
                send_sem=self.send_sems.at[number],
                recv_sem=self.recv_sems.at[number],
                device_id=device,
                device_id_type=MESH,
            ).start()
        self.open.append((number, total))
        return number, total

    def wait(self, ticket):
        number, total = ticket
        pltpu.make_async_copy(total, total, self.recv_sems.at[number]).wait()

    def finish(self):
        for number, total in self.open:
            pltpu.make_async_copy(total, total, self.send_sems.at[number]).wait()


class Exchange:
    def __init__(self, sends, replica, tensor, mask, static, bufs):
        self.sends, self.replica, self.tensor = sends, replica, tensor
        self.mask, self.static = mask, static
        self.core, self.xs, self.zs = bufs
        self.ticket = None

    def _send(self, buf, masks):
        copies = [
            (buf.at[0], buf.at[k + 1], (flip(self.replica, mask), self.tensor)) for k, mask in enumerate(masks)
        ]
        self.ticket = self.sends.start(copies, buf.at[pl.ds(1, len(masks))])

    def begin(self, payload):
        self.core[0] = payload
        if self.static is not None:
            self._send(self.core, [self.static])
        else:
            self._send(self.core, CORE_MASKS)

    def along_x(self):
        if self.static is None:
            self.sends.wait(self.ticket)
            self.xs[0] = self.core[lax.rem(self.mask, 2)]
            self._send(self.xs, X_MASKS)

    def along_z(self):
        if self.static is None:
            self.sends.wait(self.ticket)
            self.zs[0] = self.xs[lax.rem(lax.div(self.mask, 2), 4)]
            self._send(self.zs, Z_MASKS)

    def end(self):
        self.sends.wait(self.ticket)
        if self.static is not None:
            return self.core[1]
        return self.zs[lax.rem(lax.div(self.mask, 8), 4)]


def kernel(
    static, m_ref, w_hbm, h_hbm, g_hbm, s_hbm, o_hbm,
    w, h, s, gown, gf, tsend, trecv0, trecv1, tf, zsend, zrecv0, zrecv1, block, esend, erecv,
    c0, x0, z0, ce, xe, ze, df0, o0, cl, xl, zl, df1, o1, cr0, xr0, zr0, cr1, xr1, zr1,
    rd0, v, out, send_sems, recv_sems, load_sems, store_sems,
):
    replica = lax.axis_index("replica")
    tensor = lax.axis_index("tensor")
    y = lax.rem(tensor, Y)
    z = lax.div(tensor, Y)

    def at(dy, dz):
        return lax.rem(y + dy + Y, Y) + (z if dz == 0 else 1 - z) * Y

    peers = [(replica, at(dy, dz)) for dy, dz in OFFSETS]
    masks = []
    if None in static:
        masks = CORE_MASKS + X_MASKS + Z_MASKS
    masks = masks + [m for m in set(static) if m is not None]

    barrier = pltpu.get_barrier_semaphore()
    for device in peers + [(flip(replica, mask), tensor) for mask in masks]:
        pl.semaphore_signal(barrier, inc=1, device_id=device, device_id_type=MESH)

    mine = pl.ds(pl.multiple_of(tensor * 128, 128), 128)

    loads = [
        pltpu.make_async_copy(s_hbm, s, load_sems.at[0]),
        pltpu.make_async_copy(h_hbm.at[0], h, load_sems.at[1]),
        pltpu.make_async_copy(w_hbm.at[0], w, load_sems.at[2]),
        pltpu.make_async_copy(g_hbm.at[0], gown, load_sems.at[3]),
        pltpu.make_async_copy(g_hbm.at[0], gf.at[:, mine], load_sems.at[4]),
    ]
    for load in loads:
        load.start()
    loads[0].wait()
    loads[1].wait()
    tsend[...] = nt(h[...], s[...]).astype(BF)
    loads[2].wait()

    def starting_left(i, carry):
        cut = pl.ds(pl.multiple_of(i * 512, 512), 512)
        zsend[:, cut] = nn(s[...], w[:, cut]).astype(BF)
        return carry

    lax.fori_loop(0, 4, starting_left, 0)
    pl.semaphore_wait(barrier, len(peers) + len(masks))

    sends = Sends(send_sems, recv_sems)

    def scatter_tokens(step, into):
        copies = []
        for k, (r, t) in enumerate(peers):
            rows = pl.ds(pl.multiple_of(t * 16 + step * TOK, 16), 16)
            copies.append((tsend.at[rows], into.at[k], (r, t)))
        return sends.start(copies, into)

    def scatter_columns(step, into):
        copies = []
        for k, (r, t) in enumerate(peers):
            cut = pl.ds(pl.multiple_of(t * 128, 128), 128)
            copies.append((zsend.at[pl.ds(step * RANK, RANK), cut], into.at[k], (r, t)))
        return sends.start(copies, into)

    def gather_columns(source, into):
        return sends.start([(source, into.at[:, mine], p) for p in peers], into.at[:, pl.ds(0, 15 * 128)])

    def sum_tokens(step, arrived):
        rows = pl.ds(pl.multiple_of(tensor * 16 + step * TOK, 16), 16)
        total = tsend[rows].astype(F32)
        for k in range(15):
            total = total + arrived[k].astype(F32)
        tf[rows] = total.astype(BF)
        return sends.start([(tf.at[rows], tf.at[rows], p) for p in peers], tf.at[pl.ds(0, 15 * 16)])

    def sum_columns(step, arrived):
        total = zsend[pl.ds(step * RANK, RANK), mine].astype(F32)
        for k in range(15):
            total = total + arrived[k].astype(F32)
        return total

    def pumps(step):
        rows = pl.ds(step * TOK, TOK)
        ring = {}

        def shard(dy, dz, to_dy, to_dz):
            cut = pl.ds(pl.multiple_of(at(dy, dz) * 128, 128), 128)
            source = gown.at[rows] if (dy, dz) == (0, 0) else gf.at[rows, cut]
            return sends.start([(source, gf.at[rows, cut], (replica, at(to_dy, to_dz)))], gown.at[rows])

        def right(dy, dz):
            ring[dy - 1, dz] = shard(dy, dz, 1, 0)

        def left(dy, dz):
            ring[dy + 1, dz] = shard(dy, dz, -1, 0)

        def across(dy):
            ring[dy, 1] = shard(dy, 0, 0, 1)

        def arrived(dy, dz):
            sends.wait(ring.pop((dy, dz)))

        right(0, 0)
        left(0, 0)
        across(0)
        yield
        for dy in (1, 2):
            arrived(-dy, 0)
            right(-dy, 0)
            arrived(dy, 0)
            left(dy, 0)
            across(-dy)
            across(dy)
            yield
        arrived(-3, 0)
        right(-3, 0)
        arrived(-2, 1)
        right(-2, 1)
        arrived(2, 1)
        left(2, 1)
        yield
        arrived(3, 1)
        left(3, 1)
        yield
        for place in list(ring):
            arrived(*place)
        yield

    early = static[0] is not None
    rings = {"o": pumps(0), "n": pumps(1)}
    plan, right_at = PLANS[0 if early else 1]

    def pump(point):
        for name in plan[point]:
            next(rings[name])
        if point == right_at:
            part = (0.1 * nt(df0[...], gf[pl.ds(0, TOK)])).astype(BF)
            k0 = (nt(df0[...], w[...]) - nn(part, h[pl.ds(0, TOK)])).astype(BF)
            right0.begin(k0)
            return k0

    t0 = scatter_tokens(0, trecv0)
    q0 = scatter_columns(0, zrecv0)
    sends.wait(t0)
    t0 = sum_tokens(0, trecv0)
    q1 = scatter_columns(1, zrecv1)
    t1 = scatter_tokens(1, trecv1)
    loads[3].wait()
    loads[4].wait()
    pump(0)
    sends.wait(q0)
    left0 = sum_columns(0, zrecv0)
    sends.wait(t0)
    grad0 = tn(tf[pl.ds(0, TOK)], gown[pl.ds(0, TOK)])
    y0 = (left0 - 0.1 * grad0[:RANK]).astype(BF)
    first = Exchange(sends, replica, tensor, m_ref[0], static[0], (c0, x0, z0))
    cross = Exchange(sends, replica, tensor, m_ref[0], static[0], (ce, xe, ze))
    first.begin(y0)
    first.along_x()
    sends.wait(q1)
    x1 = sum_columns(1, zrecv1) - 0.1 * grad0[RANK:]
    cross.begin(x1.astype(BF))
    pump(1)
    sends.wait(t1)
    t1 = sum_tokens(1, trecv1)
    first.along_z()
    cross.along_x()
    pump(2)
    cross.along_z()
    pump(3)
    diff = (y0.astype(F32) - first.end().astype(F32)).astype(BF)
    block[0] = diff
    df0[:, mine] = diff
    d0 = gather_columns(block.at[0], df0)
    both = (x1 + cross.end().astype(F32)).astype(BF)
    mixed = nt(both, diff).astype(BF)
    mixed = jnp.concatenate([mixed[:32], mixed[32:]], axis=1)
    esend[...] = mixed
    e0 = sends.start([(esend, erecv.at[k], p) for k, p in enumerate(peers)], erecv)
    pump(4)
    sends.wait(t1)
    grad1 = tn(tf[pl.ds(TOK, TOK)], gown[pl.ds(TOK, TOK)])
    y1 = x1 - 0.09 * grad0[RANK:] - 0.1 * grad1[RANK:]
    right0 = Exchange(sends, replica, tensor, m_ref[0], static[0], (cr0, xr0, zr0))
    sends.wait(d0)
    k0 = pump(5)
    d0_all = df0[...]
    inverse0 = inverse_lower_factor(nt(d0_all, d0_all))
    o0[...] = split_nn(inverse0, d0_all).astype(BF)
    sends.wait(e0)
    mixed = mixed.astype(F32)
    for k in range(15):
        mixed = mixed + erecv[k].astype(F32)
    mixed = jnp.concatenate([mixed[:, :RANK], mixed[:, RANK:]], axis=0)
    moved = split_nt(mixed, inverse0).astype(BF)
    l1 = (y1 - 0.5 * nn(moved, o0[:, mine])).astype(BF)
    second = Exchange(sends, replica, tensor, m_ref[1], static[1], (cl, xl, zl))
    second.begin(l1)
    second.along_x()
    k0 = pump(6) if right_at == 6 else (pump(6), k0)[1]
    if right_at < 7:
        right0.along_x()
    second.along_z()
    pump(7)
    diff = (l1.astype(F32) - second.end().astype(F32)).astype(BF)
    block[1] = diff
    df1[:, mine] = diff
    d1 = gather_columns(block.at[1], df1)
    k0 = pump(8) if right_at == 8 else (pump(8), k0)[1]
    if right_at == 8:
        right0.along_x()
    right0.along_z()
    pump(9)
    sends.wait(d1)
    pump(10)
    d1_all = df1[...]
    grad_part = nt(d1_all, gf[...])
    grad_part = jnp.concatenate([0.19 * grad_part[:, :TOK], 0.1 * grad_part[:, TOK:]], axis=1).astype(BF)
    k1 = nt(d1_all, w[...]) - nn(grad_part, h[...])
    mixed = (0.5 * nt(d1_all, o0[...])).astype(BF)
    rd0[...] = split_nn(inverse0, k0.astype(F32) - right0.end().astype(F32)).astype(BF)
    k1 = (k1 - nn(mixed, rd0[...])).astype(BF)
    right1 = Exchange(sends, replica, tensor, m_ref[1], static[1], (cr1, xr1, zr1))
    right1.begin(k1)
    right1.along_x()
    inverse1 = inverse_lower_factor(nt(d1_all, d1_all))
    o1[...] = split_nn(inverse1, d1_all).astype(BF)

    def settled(i, carry):
        cut = pl.ds(pl.multiple_of(i * 256, 256), 256)
        grad = 0.19 * tn(h[pl.ds(0, TOK)], gf[pl.ds(0, TOK), cut])
        grad = grad + 0.1 * tn(h[pl.ds(TOK, TOK)], gf[pl.ds(TOK, TOK), cut])
        v[:, cut] = w[:, cut].astype(F32) - grad - 0.5 * tn(rd0[...], o0[:, cut])
        return carry

    right1.along_z()
    lax.fori_loop(0, 8, settled, 0)
    apart = k1.astype(F32) - right1.end().astype(F32)
    rd1 = split_nn(inverse1, apart).astype(BF)
    stores = []
    for i in range(4):
        rows = pl.ds(128 * i, 128)
        out[rows] = (v[rows] - 0.5 * tn(rd1[:, 128 * i : 128 * i + 128], o1[...])).astype(BF)
        store = pltpu.make_async_copy(out.at[rows], o_hbm.at[0, rows], store_sems.at[i])
        store.start()
        stores.append(store)
    sends.finish()
    for store in stores:
        store.wait()


def steps(static, number, matching, weights, hidden, out_grad, factors):
    def bf(*shape):
        return pltpu.VMEM(shape, BF)

    anywhere = pl.BlockSpec(memory_space=pl.ANY)
    return pl.pallas_call(
        functools.partial(kernel, static),
        out_shape=jax.ShapeDtypeStruct(weights.shape, BF),
        in_specs=[pl.BlockSpec(memory_space=pltpu.SMEM)] + [anywhere] * 4,
        out_specs=anywhere,
        scratch_shapes=[
            bf(512, 2048), bf(512, 512), bf(128, 512), bf(512, 128), bf(512, 2048),
            bf(512, 128), bf(15, 16, 128), bf(15, 16, 128), bf(512, 128),
            bf(128, 2048), bf(15, 64, 128), bf(15, 64, 128), bf(2, 64, 128), bf(32, 128), bf(15, 32, 128),
            bf(2, 64, 128), bf(4, 64, 128), bf(4, 64, 128), bf(2, 64, 128), bf(4, 64, 128), bf(4, 64, 128),
            bf(64, 2048), bf(64, 2048),
            bf(2, 64, 128), bf(4, 64, 128), bf(4, 64, 128), bf(64, 2048), bf(64, 2048),
            bf(2, 64, 512), bf(4, 64, 512), bf(4, 64, 512),
            bf(2, 64, 512), bf(4, 64, 512), bf(4, 64, 512),
            bf(64, 512), pltpu.VMEM((512, 2048), F32), bf(512, 2048),
            pltpu.SemaphoreType.DMA((64,)), pltpu.SemaphoreType.DMA((64,)),
            pltpu.SemaphoreType.DMA((5,)), pltpu.SemaphoreType.DMA((4,)),
        ],
        compiler_params=pltpu.CompilerParams(
            collective_id=number, has_side_effects=True, vmem_limit_bytes=60 << 20
        ),
        name="gossip_steps",
    )(matching, weights, hidden, out_grad, factors)


def per_device(weights, hidden, out_grad, factor_start, matching):
    factors = factor_start.reshape(2 * RANK, factor_start.shape[2])
    return lax.cond(
        matching[0] == 31,
        functools.partial(steps, (31, None), 0),
        functools.partial(steps, (None, 31), 1),
        matching, weights, hidden, out_grad, factors,
    )


def solution(mesh):
    return jax.shard_map(
        per_device,
        mesh=mesh,
        in_specs=(
            P("replica", "tensor", None),
            P("replica", None, "tensor"),
            P("replica", None, "tensor"),
            P(None, None, "tensor"),
            P(),
        ),
        out_specs=P("replica", "tensor", None),
        check_vma=False,
    )
```

```python
import functools

import jax
import jax.numpy as jnp
from jax import lax
from jax.experimental import pallas as pl
from jax.experimental.pallas import tpu as pltpu
from jax.sharding import PartitionSpec as P

F32 = jnp.float32
BF = jnp.bfloat16
MESH = pl.DeviceIdType.MESH
RANK = 64
TOK = 256
Y = 8
OFFSETS = [(4, 0), (3, 0), (5, 0), (2, 0), (6, 0), (4, 1), (3, 1), (5, 1), (2, 1), (6, 1), (1, 0), (7, 0), (1, 1), (7, 1), (0, 1)]
CORE_MASKS = [1]
X_MASKS = [2, 4, 6]
Z_MASKS = [8, 16, 24]


PLANS = [
    (["on", "on", "", "", "on", "", "on", "on", "on", "", ""], 8),
    (["o", "on", "on", "o", "o", "no", "n", "", "", "n", "n"], 5),
]


def flip(index, mask):
    for bit in range(5):
        if mask >> bit & 1:
            index = index + (1 - 2 * lax.rem(lax.div(index, 2**bit), 2)) * 2**bit
    return index


def nn(a, b):
    return lax.dot_general(a, b, (((1,), (0,)), ((), ())), preferred_element_type=F32)


def nt(a, b):
    return lax.dot_general(a, b, (((1,), (1,)), ((), ())), preferred_element_type=F32)


def tn(a, b):
    return lax.dot_general(a, b, (((0,), (0,)), ((), ())), preferred_element_type=F32)


def inverse_lower_factor(gram):
    n = RANK
    row_at = lax.broadcasted_iota(jnp.int32, (n, n), 0)
    col_at = lax.broadcasted_iota(jnp.int32, (n, n), 1)
    eye = (row_at == col_at).astype(F32)
    wide = jnp.concatenate([gram, eye], axis=1)
    rows = [wide[8 * j : 8 * j + 8] for j in range(8)]
    sub = lax.broadcasted_iota(jnp.int32, (8, 128), 0)

    def spread(block, s):
        return jnp.broadcast_to(block[s : s + 1, :], (8, 128))

    for jb in range(8):
        cols = [
            [jnp.broadcast_to(rows[j][:, 8 * jb + q : 8 * jb + q + 1], (8, 128)) if j >= jb else None for j in range(8)]
            for q in range(8)
        ]
        for s in range(8):
            pivot_row = spread(rows[jb], s)
            inverse = 1.0 / spread(cols[s][jb], s)
            ahead = [spread(cols[q][jb], s) if q > s else None for q in range(8)]
            for j in range(jb, 8):
                factor = cols[s][j] * inverse
                if j == jb:
                    factor = jnp.where(sub > s, factor, 0.0)
                rows[j] = rows[j] - factor * pivot_row
                for q in range(s + 1, 8):
                    cols[q][j] = cols[q][j] - factor * ahead[q]
    wide = jnp.concatenate(rows, axis=0)
    pivots = jnp.sum(wide[:, :n] * eye, axis=1, keepdims=True)
    return wide[:, n:] * lax.rsqrt(pivots)


def split(value):
    high = value.astype(BF)
    return high, (value - high.astype(F32)).astype(BF)


def split_nn(a, b):
    high, low = split(a)
    if b.dtype == BF:
        return nn(jnp.concatenate([high, low], axis=1), jnp.concatenate([b, b], axis=0))
    b_high, b_low = split(b)
    return nn(jnp.concatenate([high, low, high], axis=1), jnp.concatenate([b_high, b_high, b_low], axis=0))


def split_nt(a, b):
    a_high, a_low = split(a)
    b_high, b_low = split(b)
    return nt(jnp.concatenate([a_high, a_low, a_high], axis=1), jnp.concatenate([b_high, b_high, b_low], axis=1))


class Sends:
    def __init__(self, send_sems, recv_sems):
        self.send_sems, self.recv_sems = send_sems, recv_sems
        self.count = 0
        self.open = []

    def start(self, copies, total):
        number = self.count
        self.count += 1
        for source, target, device in copies:
            pltpu.make_async_remote_copy(
                src_ref=source,
                dst_ref=target,
                send_sem=self.send_sems.at[number],
                recv_sem=self.recv_sems.at[number],
                device_id=device,
                device_id_type=MESH,
            ).start()
        self.open.append((number, total))
        return number, total

    def wait(self, ticket):
        number, total = ticket
        pltpu.make_async_copy(total, total, self.recv_sems.at[number]).wait()

    def finish(self):
        for number, total in self.open:
            pltpu.make_async_copy(total, total, self.send_sems.at[number]).wait()


class Exchange:
    def __init__(self, sends, replica, tensor, mask, static, bufs):
        self.sends, self.replica, self.tensor = sends, replica, tensor
        self.mask, self.static = mask, static
        self.core, self.xs, self.zs = bufs
        self.ticket = None

    def _send(self, buf, masks):
        copies = [
            (buf.at[0], buf.at[k + 1], (flip(self.replica, mask), self.tensor)) for k, mask in enumerate(masks)
        ]
        self.ticket = self.sends.start(copies, buf.at[pl.ds(1, len(masks))])

    def begin(self, payload):
        self.core[0] = payload
        if self.static is not None:
            self._send(self.core, [self.static])
        else:
            self._send(self.core, CORE_MASKS)

    def along_x(self):
        if self.static is None:
            self.sends.wait(self.ticket)
            self.xs[0] = self.core[lax.rem(self.mask, 2)]
            self._send(self.xs, X_MASKS)

    def along_z(self):
        if self.static is None:
            self.sends.wait(self.ticket)
            self.zs[0] = self.xs[lax.rem(lax.div(self.mask, 2), 4)]
            self._send(self.zs, Z_MASKS)

    def end(self):
        self.sends.wait(self.ticket)
        if self.static is not None:
            return self.core[1]
        return self.zs[lax.rem(lax.div(self.mask, 8), 4)]


def kernel(
    static, m_ref, w_hbm, h_hbm, g_hbm, s_hbm, out_hbm, rd1_hbm, o1_hbm,
    w, h, s, gown, gf, tsend, trecv0, trecv1, tf, zsend, zrecv0, zrecv1, block, esend, erecv,
    c0, x0, z0, ce, xe, ze, df0, o0, cl, xl, zl, df1, o1, cr0, xr0, zr0, cr1, xr1, zr1,
    rd0, out, move, send_sems, recv_sems, load_sems, store_sems,
):
    replica = lax.axis_index("replica")
    tensor = lax.axis_index("tensor")
    y = lax.rem(tensor, Y)
    z = lax.div(tensor, Y)

    def at(dy, dz):
        return lax.rem(y + dy + Y, Y) + (z if dz == 0 else 1 - z) * Y

    peers = [(replica, at(dy, dz)) for dy, dz in OFFSETS]
    masks = []
    if None in static:
        masks = CORE_MASKS + X_MASKS + Z_MASKS
    masks = masks + [m for m in set(static) if m is not None]

    barrier = pltpu.get_barrier_semaphore()
    for device in peers + [(flip(replica, mask), tensor) for mask in masks]:
        pl.semaphore_signal(barrier, inc=1, device_id=device, device_id_type=MESH)

    mine = pl.ds(pl.multiple_of(tensor * 128, 128), 128)

    loads = [
        pltpu.make_async_copy(s_hbm, s, load_sems.at[0]),
        pltpu.make_async_copy(h_hbm.at[0], h, load_sems.at[1]),
        pltpu.make_async_copy(w_hbm.at[0], w, load_sems.at[2]),
        pltpu.make_async_copy(g_hbm.at[0], gown, load_sems.at[3]),
        pltpu.make_async_copy(g_hbm.at[0], gf.at[:, mine], load_sems.at[4]),
    ]
    for load in loads:
        load.start()
    loads[0].wait()
    loads[1].wait()
    tsend[...] = nt(h[...], s[...]).astype(BF)
    loads[2].wait()

    def starting_left(i, carry):
        cut = pl.ds(pl.multiple_of(i * 512, 512), 512)
        zsend[:, cut] = nn(s[...], w[:, cut]).astype(BF)
        return carry

    lax.fori_loop(0, 4, starting_left, 0)
    pl.semaphore_wait(barrier, len(peers) + len(masks))

    sends = Sends(send_sems, recv_sems)

    def scatter_tokens(step, into):
        copies = []
        for k, (r, t) in enumerate(peers):
            rows = pl.ds(pl.multiple_of(t * 16 + step * TOK, 16), 16)
            copies.append((tsend.at[rows], into.at[k], (r, t)))
        return sends.start(copies, into)

    def scatter_columns(step, into):
        copies = []
        for k, (r, t) in enumerate(peers):
            cut = pl.ds(pl.multiple_of(t * 128, 128), 128)
            copies.append((zsend.at[pl.ds(step * RANK, RANK), cut], into.at[k], (r, t)))
        return sends.start(copies, into)

    def gather_columns(source, into):
        return sends.start([(source, into.at[:, mine], p) for p in peers], into.at[:, pl.ds(0, 15 * 128)])

    def sum_tokens(step, arrived):
        rows = pl.ds(pl.multiple_of(tensor * 16 + step * TOK, 16), 16)
        total = tsend[rows].astype(F32)
        for k in range(15):
            total = total + arrived[k].astype(F32)
        tf[rows] = total.astype(BF)
        return sends.start([(tf.at[rows], tf.at[rows], p) for p in peers], tf.at[pl.ds(0, 15 * 16)])

    def sum_columns(step, arrived):
        total = zsend[pl.ds(step * RANK, RANK), mine].astype(F32)
        for k in range(15):
            total = total + arrived[k].astype(F32)
        return total

    def pumps(step):
        rows = pl.ds(step * TOK, TOK)
        ring = {}

        def shard(dy, dz, to_dy, to_dz):
            cut = pl.ds(pl.multiple_of(at(dy, dz) * 128, 128), 128)
            source = gown.at[rows] if (dy, dz) == (0, 0) else gf.at[rows, cut]
            return sends.start([(source, gf.at[rows, cut], (replica, at(to_dy, to_dz)))], gown.at[rows])

        def right(dy, dz):
            ring[dy - 1, dz] = shard(dy, dz, 1, 0)

        def left(dy, dz):
            ring[dy + 1, dz] = shard(dy, dz, -1, 0)

        def across(dy):
            ring[dy, 1] = shard(dy, 0, 0, 1)

        def arrived(dy, dz):
            sends.wait(ring.pop((dy, dz)))

        right(0, 0)
        left(0, 0)
        across(0)
        yield
        for dy in (1, 2):
            arrived(-dy, 0)
            right(-dy, 0)
            arrived(dy, 0)
            left(dy, 0)
            across(-dy)
            across(dy)
            yield
        arrived(-3, 0)
        right(-3, 0)
        arrived(-2, 1)
        right(-2, 1)
        arrived(2, 1)
        left(2, 1)
        yield
        arrived(3, 1)
        left(3, 1)
        yield
        for place in list(ring):
            arrived(*place)
        yield

    early = static[0] is not None
    rings = {"o": pumps(0), "n": pumps(1)}
    plan, right_at = PLANS[0 if early else 1]

    def pump(point):
        for name in plan[point]:
            next(rings[name])
        if point == right_at:
            part = (0.1 * nt(df0[...], gf[pl.ds(0, TOK)])).astype(BF)
            k0 = (nt(df0[...], w[...]) - nn(part, h[pl.ds(0, TOK)])).astype(BF)
            right0.begin(k0)
            return k0

    t0 = scatter_tokens(0, trecv0)
    q0 = scatter_columns(0, zrecv0)
    sends.wait(t0)
    t0 = sum_tokens(0, trecv0)
    q1 = scatter_columns(1, zrecv1)
    t1 = scatter_tokens(1, trecv1)
    loads[3].wait()
    loads[4].wait()
    pump(0)
    sends.wait(q0)
    left0 = sum_columns(0, zrecv0)
    sends.wait(t0)
    grad0 = tn(tf[pl.ds(0, TOK)], gown[pl.ds(0, TOK)])
    y0 = (left0 - 0.1 * grad0[:RANK]).astype(BF)
    first = Exchange(sends, replica, tensor, m_ref[0], static[0], (c0, x0, z0))
    cross = Exchange(sends, replica, tensor, m_ref[0], static[0], (ce, xe, ze))
    first.begin(y0)
    first.along_x()
    sends.wait(q1)
    x1 = sum_columns(1, zrecv1) - 0.1 * grad0[RANK:]
    cross.begin(x1.astype(BF))
    pump(1)
    sends.wait(t1)
    t1 = sum_tokens(1, trecv1)
    first.along_z()
    cross.along_x()
    pump(2)
    cross.along_z()
    pump(3)
    diff = (y0.astype(F32) - first.end().astype(F32)).astype(BF)
    block[0] = diff
    df0[:, mine] = diff
    d0 = gather_columns(block.at[0], df0)
    both = (x1 + cross.end().astype(F32)).astype(BF)
    mixed = nt(both, diff).astype(BF)
    mixed = jnp.concatenate([mixed[:32], mixed[32:]], axis=1)
    esend[...] = mixed
    e0 = sends.start([(esend, erecv.at[k], p) for k, p in enumerate(peers)], erecv)
    pump(4)
    sends.wait(t1)
    grad1 = tn(tf[pl.ds(TOK, TOK)], gown[pl.ds(TOK, TOK)])
    y1 = x1 - 0.09 * grad0[RANK:] - 0.1 * grad1[RANK:]
    right0 = Exchange(sends, replica, tensor, m_ref[0], static[0], (cr0, xr0, zr0))
    sends.wait(d0)
    k0 = pump(5)
    d0_all = df0[...]
    inverse0 = inverse_lower_factor(nt(d0_all, d0_all))
    o0[...] = split_nn(inverse0, d0_all).astype(BF)
    sends.wait(e0)
    mixed = mixed.astype(F32)
    for k in range(15):
        mixed = mixed + erecv[k].astype(F32)
    mixed = jnp.concatenate([mixed[:, :RANK], mixed[:, RANK:]], axis=0)
    moved = split_nt(mixed, inverse0).astype(BF)
    l1 = (y1 - 0.5 * nn(moved, o0[:, mine])).astype(BF)
    second = Exchange(sends, replica, tensor, m_ref[1], static[1], (cl, xl, zl))
    second.begin(l1)
    second.along_x()
    k0 = pump(6) if right_at == 6 else (pump(6), k0)[1]
    if right_at < 7:
        right0.along_x()
    second.along_z()
    pump(7)
    diff = (l1.astype(F32) - second.end().astype(F32)).astype(BF)
    block[1] = diff
    df1[:, mine] = diff
    d1 = gather_columns(block.at[1], df1)
    k0 = pump(8) if right_at == 8 else (pump(8), k0)[1]
    if right_at == 8:
        right0.along_x()
    right0.along_z()
    pump(9)
    sends.wait(d1)
    pump(10)
    d1_all = df1[...]
    grad_part = nt(d1_all, gf[...])
    grad_part = jnp.concatenate([0.19 * grad_part[:, :TOK], 0.1 * grad_part[:, TOK:]], axis=1).astype(BF)
    k1 = nt(d1_all, w[...]) - nn(grad_part, h[...])
    mixed = (0.5 * nt(d1_all, o0[...])).astype(BF)
    rd0[...] = split_nn(inverse0, k0.astype(F32) - right0.end().astype(F32)).astype(BF)
    k1 = (k1 - nn(mixed, rd0[...])).astype(BF)
    right1 = Exchange(sends, replica, tensor, m_ref[1], static[1], (cr1, xr1, zr1))
    right1.begin(k1)
    right1.along_x()
    inverse1 = inverse_lower_factor(nt(d1_all, d1_all))
    o1[...] = split_nn(inverse1, d1_all).astype(BF)

    def settled(i, carry):
        cut = pl.ds(pl.multiple_of(i * 256, 256), 256)
        grad = 0.19 * tn(h[pl.ds(0, TOK)], gf[pl.ds(0, TOK), cut])
        grad = grad + 0.1 * tn(h[pl.ds(TOK, TOK)], gf[pl.ds(TOK, TOK), cut])
        out[:, cut] = (w[:, cut].astype(F32) - grad - 0.5 * tn(rd0[...], o0[:, cut])).astype(BF)
        return carry

    right1.along_z()
    lax.fori_loop(0, 8, settled, 0)
    stores = [
        pltpu.make_async_copy(out, out_hbm.at[0], store_sems.at[0]),
        pltpu.make_async_copy(o1, o1_hbm, store_sems.at[1]),
    ]
    for store in stores:
        store.start()
    apart = k1.astype(F32) - right1.end().astype(F32)
    rd1 = split_nn(inverse1, apart).astype(BF)
    move[...] = rd1
    stores.append(pltpu.make_async_copy(move, rd1_hbm, store_sems.at[2]))
    stores[-1].start()
    sends.finish()
    for store in stores:
        store.wait()


def steps(static, number, matching, weights, hidden, out_grad, factors):
    def bf(*shape):
        return pltpu.VMEM(shape, BF)

    anywhere = pl.BlockSpec(memory_space=pl.ANY)
    return pl.pallas_call(
        functools.partial(kernel, static),
        out_shape=(
            jax.ShapeDtypeStruct(weights.shape, BF),
            jax.ShapeDtypeStruct((RANK, 512), BF),
            jax.ShapeDtypeStruct((RANK, 2048), BF),
        ),
        in_specs=[pl.BlockSpec(memory_space=pltpu.SMEM)] + [anywhere] * 4,
        out_specs=(anywhere,) * 3,
        scratch_shapes=[
            bf(512, 2048), bf(512, 512), bf(128, 512), bf(512, 128), bf(512, 2048),
            bf(512, 128), bf(15, 16, 128), bf(15, 16, 128), bf(512, 128),
            bf(128, 2048), bf(15, 64, 128), bf(15, 64, 128), bf(2, 64, 128), bf(32, 128), bf(15, 32, 128),
            bf(2, 64, 128), bf(4, 64, 128), bf(4, 64, 128), bf(2, 64, 128), bf(4, 64, 128), bf(4, 64, 128),
            bf(64, 2048), bf(64, 2048),
            bf(2, 64, 128), bf(4, 64, 128), bf(4, 64, 128), bf(64, 2048), bf(64, 2048),
            bf(2, 64, 512), bf(4, 64, 512), bf(4, 64, 512),
            bf(2, 64, 512), bf(4, 64, 512), bf(4, 64, 512),
            bf(64, 512), bf(512, 2048), bf(64, 512),
            pltpu.SemaphoreType.DMA((64,)), pltpu.SemaphoreType.DMA((64,)),
            pltpu.SemaphoreType.DMA((5,)), pltpu.SemaphoreType.DMA((4,)),
        ],
        compiler_params=pltpu.CompilerParams(
            collective_id=number, has_side_effects=True, vmem_limit_bytes=60 << 20
        ),
        name="gossip_steps",
    )(matching, weights, hidden, out_grad, factors)


def per_device(weights, hidden, out_grad, factor_start, matching):
    factors = factor_start.reshape(2 * RANK, factor_start.shape[2])
    settled, apart, ortho = lax.cond(
        matching[0] == 31,
        functools.partial(steps, (31, None), 0),
        functools.partial(steps, (None, 31), 1),
        matching, weights, hidden, out_grad, factors,
    )
    change = tn(apart, ortho)[None]
    return (settled.astype(F32) - 0.5 * change).astype(BF)


def solution(mesh):
    return jax.shard_map(
        per_device,
        mesh=mesh,
        in_specs=(
            P("replica", "tensor", None),
            P("replica", None, "tensor"),
            P("replica", None, "tensor"),
            P(None, None, "tensor"),
            P(),
        ),
        out_specs=P("replica", "tensor", None),
        check_vma=False,
    )
```
